32 devices in a mesh: gy: 2 (over y), gx: 16 (over z, x, core).
Axes of the slice: x: 2, y: 2, z: 4, core: 2. Of those that a mesh axis runs over, the one named last changes fastest.
Arguments:
- feature_grid_cells: bfloat16 [32, 256, 768], P('gy', 'gx'), may hold values from -6 to 6
- triple_mapping_matrix: bfloat16 [2, 768, 2304], replicated, may hold values from -0.21875 to 0.21875
- asker_answer_shift: float32 [2, 2, 768], replicated, may hold values from -3 to 3
- cosine_sharpness: float32 [2, 24], replicated, may hold values from 4 to 40
- offset_mlp_entry_matrix: float32 [2, 2, 512], replicated, may hold values from -5 to 5
- offset_mlp_entry_shift: float32 [2, 512], replicated, may hold values from -3 to 3
- offset_mlp_exit_matrix: float32 [2, 512, 24], replicated, may hold values from -0.25 to 0.25
- mixing_matrix: bfloat16 [2, 768, 768], replicated, may hold values from -0.21875 to 0.21875
- mixing_shift_vector: float32 [2, 768], replicated, may hold values from -3 to 3
- rescaling_gain: float32 [2, 768], replicated, may hold values from 0.25 to 1.75
- rescaling_shift: float32 [2, 768], replicated, may hold values from -3 to 3
Outputs:
- mixed: bfloat16 [32, 256, 768], P('gy', 'gx')
The draws below stay inside these ranges and needn't reach their ends.
All inputs are finite; a program needn't handle non-finite values.
Results may differ from the reference program's by a relative error of at most 0.0099.
Values may be sent and summed in bfloat16 or wider, within the bound.
A program may use at most 192 MiB of HBM per device.

```python
import math
import jax
import jax.numpy as jnp
from jax import lax

C = 768
NUM_STREAMS_ATTN = 24
WIN = 16
BIAS_NET_HIDDEN = 512
HALF_BLOCK_TOTAL = 2
H = 32
W = 256


def level_of(own_key, shape, split, least, largest):
    def one(axis_at, blocks):
        steps = jax.random.uniform(jax.random.fold_in(jax.random.fold_in(own_key, 6), axis_at), (blocks,), jnp.float32, least / len(split), largest / len(split))
        return jnp.repeat(jnp.exp(steps), shape[axis_at] // blocks).reshape((-1,) + (1,) * (len(shape) - axis_at - 1))

    factor_of = one(*split[0])
    for cut in split[1:]:
        factor_of = factor_of * one(*cut)
    return factor_of


def normal_values(stream_key, dims, width, limit, shards=(), kind=jnp.bfloat16):
    drawn = width * jax.random.normal(stream_key, dims, jnp.float32)
    if shards:
        drawn = drawn * level_of(stream_key, dims, shards, -0.22, 0.18)
    return jnp.clip(drawn, -limit, limit).astype(kind)


def setup_inputs(seed: int = 0) -> dict:
    seeds = jax.random.split(jax.random.key(seed), 12)
    return {
        "feature_grid_cells": normal_values(seeds[0], (H, W, C), 1.0, 6.0, ((0, 2), (1, 16))),
        "triple_mapping_matrix": normal_values(seeds[1], (HALF_BLOCK_TOTAL, C, 3 * C), C ** -0.5, 0.21875),
        "asker_answer_shift": normal_values(seeds[2], (HALF_BLOCK_TOTAL, 2, C), 0.5, 3.0, (), jnp.float32),
        "cosine_sharpness": jnp.clip(jnp.exp(jax.random.uniform(seeds[3], (HALF_BLOCK_TOTAL, NUM_STREAMS_ATTN), jnp.float32, math.log(4.0), math.log(40.0))), 4.0, 40.0),
        "offset_mlp_entry_matrix": normal_values(seeds[4], (HALF_BLOCK_TOTAL, 2, BIAS_NET_HIDDEN), 1.0, 5.0, (), jnp.float32),
        "offset_mlp_entry_shift": normal_values(seeds[5], (HALF_BLOCK_TOTAL, BIAS_NET_HIDDEN), 0.5, 3.0, (), jnp.float32),
        "offset_mlp_exit_matrix": normal_values(seeds[6], (HALF_BLOCK_TOTAL, BIAS_NET_HIDDEN, NUM_STREAMS_ATTN), BIAS_NET_HIDDEN ** -0.5, 0.25, (), jnp.float32),
        "mixing_matrix": normal_values(seeds[7], (HALF_BLOCK_TOTAL, C, C), C ** -0.5, 0.21875),
        "mixing_shift_vector": normal_values(seeds[8], (HALF_BLOCK_TOTAL, C), 0.5, 3.0, (), jnp.float32),
        "rescaling_gain": jnp.clip(1.0 + 0.15 * jax.random.normal(seeds[9], (HALF_BLOCK_TOTAL, C), jnp.float32), 0.25, 1.75),
        "rescaling_shift": normal_values(seeds[10], (HALF_BLOCK_TOTAL, C), 0.5, 3.0, (), jnp.float32),
    }


EPS_NORM = 1e-06
EPS_LAYER = 1e-05
MASK_VALUE = -100.0
HIGHEST = lax.Precision.HIGHEST

def stored(value):
    return lax.optimization_barrier(value.astype(jnp.bfloat16)).astype(jnp.float32)

def bias_table(w_inner, w_offset, w_outer):
    span = 2 * WIN - 1
    offsets = jnp.arange(span, dtype=jnp.float32) - (WIN - 1)
    scaled = offsets / (WIN - 1) * 8.0
    logged = jnp.sign(scaled) * jnp.log2(jnp.abs(scaled) + 1.0) / 3.0
    coords = jnp.stack([jnp.repeat(logged, span), jnp.tile(logged, span)], axis=1)
    hidden = jax.nn.relu(jnp.dot(coords, w_inner, precision=HIGHEST) + w_offset)
    bias_grid = 16.0 * jax.nn.sigmoid(jnp.dot(hidden, w_outer, precision=HIGHEST))
    bias_grid = bias_grid.T.reshape(NUM_STREAMS_ATTN, span, span)
    places = jnp.arange(WIN, dtype=jnp.int32)
    picker = (places[:, None, None] - places[None, :, None] + (WIN - 1) == jnp.arange(span, dtype=jnp.int32)[None, None, :]).astype(jnp.float32)
    row_part = jnp.einsum('hij,aci->hacj', bias_grid, picker, precision=HIGHEST)
    full_bias = jnp.einsum('hacj,bdj->habcd', row_part, picker, precision=HIGHEST)
    return full_bias.reshape(NUM_STREAMS_ATTN, WIN * WIN, WIN * WIN)

def to_windows(region):
    row_count, col_count = (region.shape[0], region.shape[1])
    trailing = region.shape[2:]
    blocked = region.reshape((row_count // WIN, WIN, col_count // WIN, WIN) + trailing)
    blocked = jnp.swapaxes(blocked, 1, 2)
    return blocked.reshape((row_count // WIN * (col_count // WIN), WIN * WIN) + trailing)

def from_windows(windows, row_count, col_count):
    trailing = windows.shape[2:]
    blocked = windows.reshape((row_count // WIN, col_count // WIN, WIN, WIN) + trailing)
    blocked = jnp.swapaxes(blocked, 1, 2)
    return blocked.reshape((row_count, col_count) + trailing)

def attend(windows, labels, displacement_additive, block_ordinal, learned_tensors):
    triple_mapping_matrix, asker_answer_shift, cosine_sharpness, mixing_matrix, mixing_shift_vector, rescaling_gain, rescaling_shift = learned_tensors
    win_count, length, channels = windows.shape
    head_dim = channels // NUM_STREAMS_ATTN
    flat = windows.reshape(win_count * length, channels)
    projected = jnp.dot(flat, triple_mapping_matrix[block_ordinal], preferred_element_type=jnp.float32)
    projected = projected.reshape(win_count, length, 3, NUM_STREAMS_ATTN, head_dim)
    biases = asker_answer_shift[block_ordinal].reshape(2, NUM_STREAMS_ATTN, head_dim)
    queries = projected[:, :, 0] + biases[0]
    key_rows = projected[:, :, 1]
    values = stored(projected[:, :, 2] + biases[1])
    queries = stored(queries * lax.rsqrt(lax.optimization_barrier(jnp.sum(queries * queries, axis=-1, keepdims=True)) + EPS_NORM))
    key_rows = stored(key_rows * lax.rsqrt(lax.optimization_barrier(jnp.sum(key_rows * key_rows, axis=-1, keepdims=True)) + EPS_NORM))
    affinity_matrix = jnp.einsum('nqhd,nkhd->nhqk', queries, key_rows, precision=HIGHEST)
    affinity_matrix = affinity_matrix * cosine_sharpness[block_ordinal][None, :, None, None] + displacement_additive[None]
    differ = (labels[:, :, None] != labels[:, None, :])[:, None]
    affinity_matrix = affinity_matrix + jnp.where(differ, MASK_VALUE, 0.0).astype(jnp.float32)
    weights = stored(jax.nn.softmax(affinity_matrix, axis=-1))
    context = jnp.einsum('nhqk,nkhd->nqhd', weights, values, precision=HIGHEST)
    context = context.astype(jnp.bfloat16).reshape(win_count * length, channels)
    branch = jnp.dot(context, mixing_matrix[block_ordinal], preferred_element_type=jnp.float32) + mixing_shift_vector[block_ordinal]
    centre = lax.optimization_barrier(jnp.mean(branch, axis=-1, keepdims=True))
    spread = lax.optimization_barrier(jnp.mean((branch - centre) ** 2, axis=-1, keepdims=True))
    normed = (branch - centre) * lax.rsqrt(spread + EPS_LAYER)
    result = flat.astype(jnp.float32) + normed * rescaling_gain[block_ordinal] + rescaling_shift[block_ordinal]
    return result.astype(jnp.bfloat16).reshape(win_count, length, channels)

def zone(position, total):
    return (position >= total - WIN).astype(jnp.int32) + (position >= total - WIN // 2).astype(jnp.int32)

def run_layer(grid, block_ordinal, learned_tensors, bias_lookup_tables, zoned):
    total_rows, total_cols, channels = grid.shape
    band_count = total_rows // WIN
    per_band = total_cols // WIN
    displacement_additive = bias_table(bias_lookup_tables[0][block_ordinal], bias_lookup_tables[1][block_ordinal], bias_lookup_tables[2][block_ordinal])
    windows = to_windows(grid).reshape(band_count, per_band, WIN * WIN, channels)
    if zoned:
        row_zone = zone(jnp.arange(total_rows, dtype=jnp.int32), total_rows)
        col_zone = zone(jnp.arange(total_cols, dtype=jnp.int32), total_cols)
        labels = 3 * row_zone[:, None] + col_zone[None, :]
    else:
        labels = jnp.zeros((total_rows, total_cols), jnp.int32)
    win_labels = to_windows(labels).reshape(band_count, per_band, WIN * WIN)
    outputs = lax.map(lambda pair: attend(pair[0], pair[1], displacement_additive, block_ordinal, learned_tensors), (windows, win_labels))
    return from_windows(outputs.reshape(band_count * per_band, WIN * WIN, channels), total_rows, total_cols)

def reference(feature_grid_cells, triple_mapping_matrix, asker_answer_shift, cosine_sharpness, offset_mlp_entry_matrix, offset_mlp_entry_shift, offset_mlp_exit_matrix, mixing_matrix, mixing_shift_vector, rescaling_gain, rescaling_shift):
    learned_tensors = (triple_mapping_matrix, asker_answer_shift, cosine_sharpness, mixing_matrix, mixing_shift_vector, rescaling_gain, rescaling_shift)
    bias_lookup_tables = (offset_mlp_entry_matrix, offset_mlp_entry_shift, offset_mlp_exit_matrix)
    half_win = WIN // 2
    first_out = run_layer(feature_grid_cells, 0, learned_tensors, bias_lookup_tables, False)
    rolled = jnp.roll(first_out, (-half_win, -half_win), (0, 1))
    rolled_out = run_layer(rolled, 1, learned_tensors, bias_lookup_tables, True)
    return jnp.roll(rolled_out, (half_win, half_win), (0, 1))
```

```python
import functools

import jax
import jax.numpy as jnp
from jax import lax
from jax.experimental import pallas as pl
from jax.experimental.pallas import tpu as pltpu
from jax.sharding import PartitionSpec as P

HEADS = 24
WIN = 16
HALF = WIN // 2
TOKENS = WIN * WIN
QUARTER = HALF * HALF
HEAD_DIM = 32
PACK = 4
LANES = PACK * HEAD_DIM
SPAN = 2 * WIN - 1
EPS_NORM = 1e-06
EPS_LAYER = 1e-05
LOG2E = 1.4426950408889634
MASK2 = 100.0 * LOG2E
CENTRE = 8.0
MESH = pl.DeviceIdType.MESH
F32 = jnp.float32
BF16 = jnp.bfloat16


def iota(shape, dim):
    return lax.broadcasted_iota(jnp.int32, shape, dim)


def coordinate(offset):
    scaled = offset / (WIN - 1) * 8.0
    magnitude = jnp.log(jnp.abs(scaled) + 1.0) * (LOG2E / 3.0)
    return jnp.where(scaled < 0.0, -magnitude, magnitude)


def split_two(x):
    hi = x.astype(BF16)
    return hi, (x - hi.astype(F32)).astype(BF16)


def bias_strips(block, w_in_ref, w_off_ref, w_out_ref, table_ref):
    hidden_width = w_in_ref.shape[2]
    w0 = w_in_ref[block, 0:1, :]
    w1 = w_in_ref[block, 1:2, :]
    shift = w_off_ref[block : block + 1, :]
    w_hi, w_lo = split_two(w_out_ref[block])
    u = coordinate((WIN - 1) - iota((2 * WIN, 1), 0).astype(F32))
    row_term = u * w0 + shift
    for part in range(2):
        e = iota((WIN, 1), 0).astype(F32) + float(part * WIN)
        col_term = coordinate((WIN - 1) - e) * w1
        for piece in range(2):
            rows = [
                jnp.maximum(row_term[i : i + 1, :] + col_term, 0.0)
                for i in range(piece * WIN, (piece + 1) * WIN)
            ]
            h_hi, h_lo = split_two(jnp.concatenate(rows, axis=0))
            dims = (((1,), (1,)), ((), ()))
            out = lax.dot_general(w_hi, h_hi, dims, preferred_element_type=F32)
            out = out + lax.dot_general(w_hi, h_lo, dims, preferred_element_type=F32)
            out = out + lax.dot_general(w_lo, h_hi, dims, preferred_element_type=F32)
            value = 16.0 * LOG2E / (1.0 + jnp.exp2(out * -LOG2E)) - CENTRE * LOG2E
            first = part * 512 + piece * 256
            table_ref[:, first : first + 256] = value


def bias_expand(table_ref, bias_ref, mask_add):
    b_row = iota((WIN, 512), 0)
    d_col = iota((WIN, 512), 1) % WIN
    near = d_col <= b_row

    @pl.loop(0, HEADS)
    def _(h):
        x1 = jnp.broadcast_to(table_ref[pl.ds(h, 1), 0:512], (WIN, 512))
        x2 = jnp.broadcast_to(table_ref[pl.ds(h, 1), 512:1024], (WIN, 512))
        r1 = pltpu.roll(x1, 512 - (WIN - 1), 1, stride=1, stride_axis=0)
        r2 = pltpu.roll(x2, 1, 1, stride=1, stride_axis=0)
        strip = jnp.where(near, r1, r2)
        for a in range(HALF):
            m = 7 - a
            rolled = strip if m == 0 else pltpu.roll(strip, 512 - 16 * m, 1)
            piece = rolled[:, 0:384]
            if mask_add is not None:
                piece = piece + mask_add
            bias_ref[h, a * WIN : (a + 1) * WIN, :] = piece


def project(block, x_rows, w_ref, shift_ref, sharp_ref, q_ref, k_ref, v_ref):
    channels = x_rows.shape[1]
    same = (iota((256, 256), 0) // HEAD_DIM == iota((256, 256), 1) // HEAD_DIM).astype(BF16)
    lane_head = iota((1, LANES), 1) // HEAD_DIM
    for piece in range(channels // 256):
        for kind in range(3):
            first = kind * channels + piece * 256
            z = jnp.dot(x_rows, w_ref[:, first : first + 256], preferred_element_type=F32)
            here = slice(piece * 256, piece * 256 + 256)
            if kind == 0:
                z = z + shift_ref[block, 0:1, here]
            if kind == 2:
                z = z + shift_ref[block, 1:2, here]
            else:
                total = jnp.dot((z * z).astype(BF16), same, preferred_element_type=F32)
                z = z * lax.rsqrt(total + EPS_NORM)
            for half in range(2):
                group = piece * 2 + half
                part = z[:, half * LANES : (half + 1) * LANES]
                if kind == 0:
                    scale = jnp.zeros((1, LANES), F32)
                    for j in range(PACK):
                        scale = jnp.where(lane_head == j, sharp_ref[block, group * PACK + j], scale)
                    part = part * (scale * LOG2E)
                target = (q_ref, k_ref, v_ref)[kind]
                target[group] = part.astype(BF16)


def attention(q_ref, k_ref, v_ref, bias_ref, ctx_ref):
    lane_head = iota((1, LANES), 1) // HEAD_DIM

    @pl.loop(0, HEADS // PACK)
    def _(g):
        q = q_ref[g]
        k = k_ref[g]
        v = v_ref[g]
        weights, values = [], []
        for j in range(PACK):
            own = (lane_head == j).astype(BF16)
            scores = lax.dot_general(
                q, k * own, (((1,), (1,)), ((), ())), preferred_element_type=F32
            )
            h = g * PACK + j
            top = jnp.exp2(scores[:128] + bias_ref[h, :, 128:384]).astype(BF16)
            low = jnp.exp2(scores[128:] + bias_ref[h, :, 0:256]).astype(BF16)
            weights.append(jnp.concatenate([top, low], axis=0))
            values.append(jnp.concatenate([v * own, jnp.broadcast_to(own, v.shape)], axis=1))
        both = jnp.dot(
            jnp.concatenate(weights, axis=1),
            jnp.concatenate(values, axis=0),
            preferred_element_type=F32,
        )
        ctx_ref[g] = (both[:, :LANES] / both[:, LANES:]).astype(BF16)


def mix_and_norm(block, x_rows, ctx_ref, w_ref, add_ref, gain_ref, shift_ref):
    groups = ctx_ref.shape[0]
    ctx = jnp.concatenate([ctx_ref[g] for g in range(groups)], axis=1)
    branch = jnp.dot(ctx, w_ref[...], preferred_element_type=F32) + add_ref[block : block + 1, :]
    branch = branch - jnp.mean(branch, axis=-1, keepdims=True)
    spread = jnp.mean(branch * branch, axis=-1, keepdims=True)
    normed = branch * lax.rsqrt(spread + EPS_LAYER)
    return x_rows.astype(F32) + normed * gain_ref[block : block + 1, :] + shift_ref[block : block + 1, :]


def quadrants(rows):
    channels = rows.shape[1]
    grid = rows.reshape(2, HALF, 2, HALF, channels)
    return [
        jnp.concatenate([grid[i, r, j] for r in range(HALF)], axis=0)
        for i in range(2)
        for j in range(2)
    ]


def from_quadrants(parts):
    channels = parts[0].shape[1]
    rows = []
    for i in range(2):
        for r in range(HALF):
            for j in range(2):
                rows.append(parts[2 * i + j][r * HALF : (r + 1) * HALF, :])
    return jnp.concatenate(rows, axis=0)


def body(
    ny,
    nx,
    x_ref,
    w_qkv_hbm,
    qv_shift_ref,
    sharp_ref,
    w_in_ref,
    w_off_ref,
    w_out_ref,
    w_mix_hbm,
    mix_add_ref,
    gain_ref,
    shift_ref,
    out_ref,
    w_qkv_ref,
    w_mix_ref,
    table_ref,
    bias_ref,
    q_ref,
    k_ref,
    v_ref,
    ctx_ref,
    send_ref,
    window_ref,
    back_ref,
    home_ref,
    w_sem,
    send_sem,
    recv_sem,
    back_send_sem,
    back_recv_sem,
):
    gy = lax.axis_index("gy")
    gx = lax.axis_index("gx")
    prev_y, next_y = lax.rem(gy + ny - 1, ny), lax.rem(gy + 1, ny)
    prev_x, next_x = lax.rem(gx + nx - 1, nx), lax.rem(gx + 1, nx)
    givers = {1: (gy, prev_x), 2: (prev_y, gx), 3: (prev_y, prev_x)}
    takers = {1: (gy, next_x), 2: (next_y, gx), 3: (next_y, next_x)}

    barrier = pltpu.get_barrier_semaphore()
    for device in list(givers.values()) + list(takers.values()):
        pl.semaphore_signal(barrier, inc=1, device_id=device, device_id_type=MESH)

    loads = []
    for block in range(2):
        loads.append(
            (
                pltpu.make_async_copy(w_qkv_hbm.at[block], w_qkv_ref.at[block], w_sem.at[2 * block]),
                pltpu.make_async_copy(w_mix_hbm.at[block], w_mix_ref.at[block], w_sem.at[2 * block + 1]),
            )
        )
    for pair in loads:
        pair[0].start()
        pair[1].start()

    bias_strips(0, w_in_ref, w_off_ref, w_out_ref, table_ref)
    bias_expand(table_ref, bias_ref, None)
    loads[0][0].wait()
    x = x_ref[...]
    project(0, x, w_qkv_ref.at[0], qv_shift_ref, sharp_ref, q_ref, k_ref, v_ref)
    attention(q_ref, k_ref, v_ref, bias_ref, ctx_ref)
    loads[0][1].wait()
    first = mix_and_norm(0, x, ctx_ref, w_mix_ref.at[0], mix_add_ref, gain_ref, shift_ref)
    parts = quadrants(first)
    window_ref[0] = parts[3].astype(BF16)
    send_ref[0] = parts[2].astype(BF16)
    send_ref[1] = parts[1].astype(BF16)
    send_ref[2] = parts[0].astype(BF16)
    pl.semaphore_wait(barrier, 6)
    out_copies = [
        pltpu.make_async_remote_copy(
            src_ref=send_ref.at[n - 1],
            dst_ref=window_ref.at[n],
            send_sem=send_sem.at[n - 1],
            recv_sem=recv_sem.at[n - 1],
            device_id=givers[n],
            device_id_type=MESH,
        )
        for n in (1, 2, 3)
    ]
    for copy in out_copies:
        copy.start()

    bias_strips(1, w_in_ref, w_off_ref, w_out_ref, table_ref)
    b_low = iota((WIN, 384), 0) < HALF
    lane = iota((WIN, 384), 1)
    d_low = lane % WIN < HALF
    col_differs = jnp.where(b_low != d_low, 1, 0) * (gx == nx - 1).astype(jnp.int32)
    row_differs = jnp.where((lane < 128) | (lane >= 256), 1, 0) * (gy == ny - 1).astype(jnp.int32)
    mask_add = jnp.where(col_differs + row_differs > 0, -MASK2, 0.0)
    bias_expand(table_ref, bias_ref, mask_add)
    loads[1][0].wait()
    for copy in out_copies:
        copy.wait()

    x = from_quadrants([window_ref[n].astype(F32) for n in range(4)]).astype(BF16)
    project(1, x, w_qkv_ref.at[1], qv_shift_ref, sharp_ref, q_ref, k_ref, v_ref)
    attention(q_ref, k_ref, v_ref, bias_ref, ctx_ref)
    loads[1][1].wait()
    second = mix_and_norm(1, x, ctx_ref, w_mix_ref.at[1], mix_add_ref, gain_ref, shift_ref)
    parts = quadrants(second)
    for n in (1, 2, 3):
        back_ref[n - 1] = parts[n].astype(BF16)
    back_copies = [
        pltpu.make_async_remote_copy(
            src_ref=back_ref.at[n - 1],
            dst_ref=home_ref.at[n - 1],
            send_sem=back_send_sem.at[n - 1],
            recv_sem=back_recv_sem.at[n - 1],
            device_id=takers[n],
            device_id_type=MESH,
        )
        for n in (1, 2, 3)
    ]
    for copy in back_copies:
        copy.start()
    for copy in back_copies:
        copy.wait()
    home = [home_ref[2].astype(F32), home_ref[1].astype(F32), home_ref[0].astype(F32), parts[0]]
    out_ref[...] = from_quadrants(home).astype(BF16)


def on_device(x, w_qkv, qv_shift, sharp, w_in, w_off, w_out, w_mix, mix_add, gain, shift):
    rows, cols, channels = x.shape
    groups = HEADS // PACK
    vmem = pl.BlockSpec(memory_space=pltpu.VMEM)
    smem = pl.BlockSpec(memory_space=pltpu.SMEM)
    hbm = pl.BlockSpec(memory_space=pl.ANY)
    kernel = functools.partial(body, lax.axis_size("gy"), lax.axis_size("gx"))
    out = pl.pallas_call(
        kernel,
        out_shape=jax.ShapeDtypeStruct((rows * cols, channels), BF16),
        in_specs=[vmem, hbm, vmem, smem, vmem, vmem, vmem, hbm, vmem, vmem, vmem],
        out_specs=vmem,
        scratch_shapes=[
            pltpu.VMEM(w_qkv.shape, BF16),
            pltpu.VMEM(w_mix.shape, BF16),
            pltpu.VMEM((HEADS, 1024), F32),
            pltpu.VMEM((HEADS, 128, 384), F32),
            pltpu.VMEM((groups, TOKENS, LANES), BF16),
            pltpu.VMEM((groups, TOKENS, LANES), BF16),
            pltpu.VMEM((groups, TOKENS, LANES), BF16),
            pltpu.VMEM((groups, TOKENS, LANES), BF16),
            pltpu.VMEM((3, QUARTER, channels), BF16),
            pltpu.VMEM((4, QUARTER, channels), BF16),
            pltpu.VMEM((3, QUARTER, channels), BF16),
            pltpu.VMEM((3, QUARTER, channels), BF16),
            pltpu.SemaphoreType.DMA((4,)),
            pltpu.SemaphoreType.DMA((3,)),
            pltpu.SemaphoreType.DMA((3,)),
            pltpu.SemaphoreType.DMA((3,)),
            pltpu.SemaphoreType.DMA((3,)),
        ],
        compiler_params=pltpu.CompilerParams(
            collective_id=0, has_side_effects=True, vmem_limit_bytes=56 * 1024 * 1024
        ),
    )(
        x.reshape(rows * cols, channels),
        w_qkv,
        qv_shift,
        sharp,
        w_in,
        w_off,
        jnp.swapaxes(w_out, 1, 2),
        w_mix,
        mix_add,
        gain,
        shift,
    )
    return out.reshape(rows, cols, channels)


def solution(mesh):
    in_specs = (P("gy", "gx", None), P(), P(), P(), P(), P(), P(), P(), P(), P(), P())
    return jax.shard_map(
        on_device, mesh=mesh, in_specs=in_specs, out_specs=P("gy", "gx", None), check_vma=False
    )
```

```python
import functools

import jax
import jax.numpy as jnp
from jax import lax
from jax.experimental import pallas as pl
from jax.experimental.pallas import tpu as pltpu
from jax.sharding import PartitionSpec as P

HEADS = 24
WIN = 16
HALF = WIN // 2
TOKENS = WIN * WIN
QUARTER = HALF * HALF
HEAD_DIM = 32
PACK = 4
LANES = PACK * HEAD_DIM
SPAN = 2 * WIN - 1
EPS_NORM = 1e-06
EPS_LAYER = 1e-05
LOG2E = 1.4426950408889634
MASK2 = 100.0 * LOG2E
CENTRE = 8.0
FIXED = 4095.0
MESH = pl.DeviceIdType.MESH
F32 = jnp.float32
BF16 = jnp.bfloat16


def iota(shape, dim):
    return lax.broadcasted_iota(jnp.int32, shape, dim)


def coordinate(offset):
    scaled = offset / (WIN - 1) * 8.0
    magnitude = jnp.log(jnp.abs(scaled) + 1.0) * (LOG2E / 3.0)
    return jnp.where(scaled < 0.0, -magnitude, magnitude)


def split_two(x):
    hi = x.astype(BF16)
    return hi, (x - hi.astype(F32)).astype(BF16)


def bias_strips(block, w_in_ref, w_off_ref, w_out_ref, table_ref):
    w0 = w_in_ref[block, 0:1, :]
    w1 = w_in_ref[block, 1:2, :]
    shift = w_off_ref[block : block + 1, :]
    w_out = w_out_ref[block]
    heads = w_out.shape[0]
    w_hi, w_lo = split_two(w_out)
    w_both = jnp.concatenate([w_hi.astype(F32), w_lo.astype(F32)], axis=0).astype(BF16)
    u = coordinate((WIN - 1) - iota((2 * WIN, 1), 0).astype(F32))
    row_term = u * w0 + shift
    dims = (((1,), (1,)), ((), ()))
    for piece in range(2):
        fixed = []
        for part in range(2):
            e = iota((WIN, 1), 0).astype(F32) + float(part * WIN)
            col_term = coordinate((WIN - 1) - e) * w1
            rows = []
            for i in range(piece * WIN, (piece + 1) * WIN):
                at = (i - part) % (2 * WIN)
                rows.append(jnp.maximum(row_term[at : at + 1, :] + col_term, 0.0))
            h_hi, h_lo = split_two(jnp.concatenate(rows, axis=0))
            both = lax.dot_general(w_both, h_hi, dims, preferred_element_type=F32)
            out = lax.dot_general(w_hi, h_lo, dims, preferred_element_type=F32)
            out = out + both[:heads] + both[heads:]
            value = 16.0 / (1.0 + jnp.exp2(out * -LOG2E)) - CENTRE
            fixed.append(jnp.round(value * FIXED).astype(jnp.int32))
        table_ref[:, piece * 256 : piece * 256 + 256] = (fixed[0] << 16) | (fixed[1] & 0xFFFF)


def expand_head(table_ref, bias_ref, h, mask_add):
    b_row = iota((WIN, 512), 0)
    near = iota((WIN, 512), 1) % WIN <= b_row
    x = jnp.broadcast_to(table_ref[pl.ds(h, 1), :], (WIN, 512))
    r = pltpu.roll(x, 512 - (WIN - 1), 1, stride=1, stride_axis=0)
    strip = jnp.where(near, r, r << 16)
    pair = (strip[:HALF] & -65536) | lax.shift_right_logical(strip[HALF:], 16)
    for a in range(HALF):
        m = 7 - a
        rolled = pair if m == 0 else pltpu.roll(pair, 512 - 16 * m, 1)
        rolled = rolled[:, 0:384]
        first = (rolled >> 16).astype(F32) * (LOG2E / FIXED)
        second = ((rolled << 16) >> 16).astype(F32) * (LOG2E / FIXED)
        if mask_add is not None:
            first = first + mask_add[:HALF]
            second = second + mask_add[HALF:]
        bias_ref[h, a * WIN : a * WIN + HALF, :] = first
        bias_ref[h, a * WIN + HALF : (a + 1) * WIN, :] = second


def bias_expand(table_ref, bias_ref, mask_add):
    @pl.loop(0, HEADS, unroll=8)
    def _(h):
        expand_head(table_ref, bias_ref, h, mask_add)


def project(block, x_rows, w_ref, shift_ref, sharp_ref, q_ref, k_ref, v_ref):
    channels = x_rows.shape[1]
    same = (iota((256, 256), 0) // HEAD_DIM == iota((256, 256), 1) // HEAD_DIM).astype(BF16)
    lane_head = iota((1, LANES), 1) // HEAD_DIM
    for piece in range(channels // 256):
        for kind in range(3):
            first = kind * channels + piece * 256
            z = jnp.dot(x_rows, w_ref[:, first : first + 256], preferred_element_type=F32)
            here = slice(piece * 256, piece * 256 + 256)
            if kind == 0:
                z = z + shift_ref[block, 0:1, here]
            if kind == 2:
                z = z + shift_ref[block, 1:2, here]
            else:
                total = jnp.dot((z * z).astype(BF16), same, preferred_element_type=F32)
                z = z * lax.rsqrt(total + EPS_NORM)
            for half in range(2):
                group = piece * 2 + half
                part = z[:, half * LANES : (half + 1) * LANES]
                if kind == 0:
                    scale = jnp.zeros((1, LANES), F32)
                    for j in range(PACK):
                        scale = jnp.where(lane_head == j, sharp_ref[block, group * PACK + j], scale)
                    part = part * (scale * LOG2E)
                target = (q_ref, k_ref, v_ref)[kind]
                target[group] = part.astype(BF16)


def attention(q_ref, k_ref, v_ref, bias_ref, ctx_ref):
    lane_head = iota((1, LANES), 1) // HEAD_DIM

    @pl.loop(0, HEADS // PACK, unroll=HEADS // PACK)
    def _(g):
        q = q_ref[g]
        k = k_ref[g]
        v = v_ref[g]
        weights, values = [], []
        for j in range(PACK):
            own = (lane_head == j).astype(BF16)
            scores = lax.dot_general(
                q, k * own, (((1,), (1,)), ((), ())), preferred_element_type=F32
            )
            h = g * PACK + j
            top = jnp.exp2(scores[:128] + bias_ref[h, :, 128:384]).astype(BF16)
            low = jnp.exp2(scores[128:] + bias_ref[h, :, 0:256]).astype(BF16)
            weights.append(jnp.concatenate([top, low], axis=0))
            values.append(jnp.concatenate([v * own, jnp.broadcast_to(own, v.shape)], axis=1))
        both = jnp.dot(
            jnp.concatenate(weights, axis=1),
            jnp.concatenate(values, axis=0),
            preferred_element_type=F32,
        )
        ctx_ref[g] = (both[:, :LANES] / both[:, LANES:]).astype(BF16)


def mix_and_norm(block, x_rows, ctx_ref, w_ref, add_ref, gain_ref, shift_ref):
    groups = ctx_ref.shape[0]
    ctx = jnp.concatenate([ctx_ref[g] for g in range(groups)], axis=1)
    branch = jnp.dot(ctx, w_ref[...], preferred_element_type=F32) + add_ref[block : block + 1, :]
    branch = branch - jnp.mean(branch, axis=-1, keepdims=True)
    spread = jnp.mean(branch * branch, axis=-1, keepdims=True)
    normed = branch * lax.rsqrt(spread + EPS_LAYER)
    return x_rows.astype(F32) + normed * gain_ref[block : block + 1, :] + shift_ref[block : block + 1, :]


def quadrants(rows):
    channels = rows.shape[1]
    grid = rows.reshape(2, HALF, 2, HALF, channels)
    return [
        jnp.concatenate([grid[i, r, j] for r in range(HALF)], axis=0)
        for i in range(2)
        for j in range(2)
    ]


def from_quadrants(parts):
    channels = parts[0].shape[1]
    rows = []
    for i in range(2):
        for r in range(HALF):
            for j in range(2):
                rows.append(parts[2 * i + j][r * HALF : (r + 1) * HALF, :])
    return jnp.concatenate(rows, axis=0)


def body(
    ny,
    nx,
    x_ref,
    w_qkv_hbm,
    qv_shift_ref,
    sharp_ref,
    w_in_ref,
    w_off_ref,
    w_out_ref,
    w_mix_hbm,
    mix_add_ref,
    gain_ref,
    shift_ref,
    out_ref,
    w_qkv_ref,
    w_mix_ref,
    table_ref,
    bias_ref,
    q_ref,
    k_ref,
    v_ref,
    ctx_ref,
    send_ref,
    window_ref,
    back_ref,
    w_sem,
    send_sem,
    recv_sem,
    back_send_sem,
    back_recv_sem,
):
    gy = lax.axis_index("gy")
    gx = lax.axis_index("gx")
    prev_y, next_y = lax.rem(gy + ny - 1, ny), lax.rem(gy + 1, ny)
    prev_x, next_x = lax.rem(gx + nx - 1, nx), lax.rem(gx + 1, nx)
    givers = {1: (gy, prev_x), 2: (prev_y, gx), 3: (prev_y, prev_x)}
    takers = {1: (gy, next_x), 2: (next_y, gx), 3: (next_y, next_x)}

    barrier = pltpu.get_barrier_semaphore()
    for device in list(givers.values()) + list(takers.values()):
        pl.semaphore_signal(barrier, inc=1, device_id=device, device_id_type=MESH)

    loads = []
    for block in range(2):
        loads.append(
            (
                pltpu.make_async_copy(w_qkv_hbm.at[block], w_qkv_ref.at[block], w_sem.at[2 * block]),
                pltpu.make_async_copy(w_mix_hbm.at[block], w_mix_ref.at[block], w_sem.at[2 * block + 1]),
            )
        )
    for pair in loads:
        pair[0].start()
        pair[1].start()

    bias_strips(0, w_in_ref, w_off_ref, w_out_ref, table_ref)
    bias_expand(table_ref, bias_ref, None)
    loads[0][0].wait()
    x = x_ref[...]
    project(0, x, w_qkv_ref.at[0], qv_shift_ref, sharp_ref, q_ref, k_ref, v_ref)
    attention(q_ref, k_ref, v_ref, bias_ref, ctx_ref)
    loads[0][1].wait()
    first = mix_and_norm(0, x, ctx_ref, w_mix_ref.at[0], mix_add_ref, gain_ref, shift_ref)
    parts = quadrants(first)
    window_ref[0] = parts[3].astype(BF16)
    send_ref[0] = parts[2].astype(BF16)
    send_ref[1] = parts[1].astype(BF16)
    send_ref[2] = parts[0].astype(BF16)
    pl.semaphore_wait(barrier, 6)
    out_copies = [
        pltpu.make_async_remote_copy(
            src_ref=send_ref.at[n - 1],
            dst_ref=window_ref.at[n],
            send_sem=send_sem.at[n - 1],
            recv_sem=recv_sem.at[n - 1],
            device_id=givers[n],
            device_id_type=MESH,
        )
        for n in (1, 2, 3)
    ]
    for copy in out_copies:
        copy.start()

    bias_strips(1, w_in_ref, w_off_ref, w_out_ref, table_ref)
    b_low = iota((WIN, 384), 0) < HALF
    lane = iota((WIN, 384), 1)
    d_low = lane % WIN < HALF
    col_differs = jnp.where(b_low != d_low, 1, 0) * (gx == nx - 1).astype(jnp.int32)
    row_differs = jnp.where((lane < 128) | (lane >= 256), 1, 0) * (gy == ny - 1).astype(jnp.int32)
    mask_add = jnp.where(col_differs + row_differs > 0, -MASK2, 0.0)
    bias_expand(table_ref, bias_ref, mask_add)
    loads[1][0].wait()
    for copy in out_copies:
        copy.wait()

    x = from_quadrants([window_ref[n].astype(F32) for n in range(4)]).astype(BF16)
    project(1, x, w_qkv_ref.at[1], qv_shift_ref, sharp_ref, q_ref, k_ref, v_ref)
    attention(q_ref, k_ref, v_ref, bias_ref, ctx_ref)
    loads[1][1].wait()
    second = mix_and_norm(1, x, ctx_ref, w_mix_ref.at[1], mix_add_ref, gain_ref, shift_ref)
    parts = quadrants(second)
    for n in range(4):
        back_ref[n] = parts[n].astype(BF16)
    back_copies = [
        pltpu.make_async_remote_copy(
            src_ref=back_ref.at[n],
            dst_ref=out_ref.at[3 - n],
            send_sem=back_send_sem.at[n],
            recv_sem=back_recv_sem.at[n],
            device_id=takers[n],
            device_id_type=MESH,
        )
        for n in (1, 2, 3)
    ]
    for copy in back_copies:
        copy.start()
    keep = pltpu.make_async_copy(back_ref.at[0], out_ref.at[3], back_send_sem.at[0])
    keep.start()
    for copy in back_copies:
        copy.wait()
    keep.wait()


def on_device(x, w_qkv, qv_shift, sharp, w_in, w_off, w_out, w_mix, mix_add, gain, shift):
    rows, cols, channels = x.shape
    groups = HEADS // PACK
    vmem = pl.BlockSpec(memory_space=pltpu.VMEM)
    smem = pl.BlockSpec(memory_space=pltpu.SMEM)
    hbm = pl.BlockSpec(memory_space=pl.ANY)
    kernel = functools.partial(body, lax.axis_size("gy"), lax.axis_size("gx"))
    out = pl.pallas_call(
        kernel,
        out_shape=jax.ShapeDtypeStruct((4, QUARTER, channels), BF16),
        in_specs=[vmem, hbm, vmem, smem, vmem, vmem, vmem, hbm, vmem, vmem, vmem],
        out_specs=hbm,
        scratch_shapes=[
            pltpu.VMEM(w_qkv.shape, BF16),
            pltpu.VMEM(w_mix.shape, BF16),
            pltpu.VMEM((HEADS, 512), jnp.int32),
            pltpu.VMEM((HEADS, 128, 384), F32),
            pltpu.VMEM((groups, TOKENS, LANES), BF16),
            pltpu.VMEM((groups, TOKENS, LANES), BF16),
            pltpu.VMEM((groups, TOKENS, LANES), BF16),
            pltpu.VMEM((groups, TOKENS, LANES), BF16),
            pltpu.VMEM((3, QUARTER, channels), BF16),
            pltpu.VMEM((4, QUARTER, channels), BF16),
            pltpu.VMEM((4, QUARTER, channels), BF16),
            pltpu.SemaphoreType.DMA((4,)),
            pltpu.SemaphoreType.DMA((3,)),
            pltpu.SemaphoreType.DMA((3,)),
            pltpu.SemaphoreType.DMA((4,)),
            pltpu.SemaphoreType.DMA((4,)),
        ],
        compiler_params=pltpu.CompilerParams(
            collective_id=0, has_side_effects=True, vmem_limit_bytes=56 * 1024 * 1024
        ),
    )(
        x.reshape(rows * cols, channels),
        w_qkv,
        qv_shift,
        sharp,
        w_in,
        w_off,
        jnp.swapaxes(w_out, 1, 2),
        w_mix,
        mix_add,
        gain,
        shift,
    )
    out = out.reshape(2, 2, HALF, HALF, channels).transpose(0, 2, 1, 3, 4)
    return out.reshape(rows, cols, channels)


def solution(mesh):
    in_specs = (P("gy", "gx", None), P(), P(), P(), P(), P(), P(), P(), P(), P(), P())
    return jax.shard_map(
        on_device, mesh=mesh, in_specs=in_specs, out_specs=P("gy", "gx", None), check_vma=False
    )
```

```python
import functools

import jax
import jax.numpy as jnp
from jax import lax
from jax.experimental import pallas as pl
from jax.experimental.pallas import tpu as pltpu
from jax.sharding import PartitionSpec as P

HEADS = 24
WIN = 16
HALF = WIN // 2
TOKENS = WIN * WIN
QUARTER = HALF * HALF
HEAD_DIM = 32
PACK = 4
LANES = PACK * HEAD_DIM
SPAN = 2 * WIN - 1
EPS_NORM = 1e-06
EPS_LAYER = 1e-05
LOG2E = 1.4426950408889634
MASK2 = 100.0 * LOG2E
CENTRE = 8.0
FIXED = 4095.0
MESH = pl.DeviceIdType.MESH
F32 = jnp.float32
BF16 = jnp.bfloat16


def iota(shape, dim):
    return lax.broadcasted_iota(jnp.int32, shape, dim)


def coordinate(offset):
    scaled = offset / (WIN - 1) * 8.0
    magnitude = jnp.log(jnp.abs(scaled) + 1.0) * (LOG2E / 3.0)
    return jnp.where(scaled < 0.0, -magnitude, magnitude)


def split_two(x):
    hi = x.astype(BF16)
    return hi, (x - hi.astype(F32)).astype(BF16)


def bias_strips(block, w_in_ref, w_off_ref, w_out_ref, table_ref):
    w0 = w_in_ref[block, 0:1, :]
    w1 = w_in_ref[block, 1:2, :]
    shift = w_off_ref[block : block + 1, :]
    w_out = w_out_ref[block]
    heads = w_out.shape[0]
    w_hi, w_lo = split_two(w_out)
    w_both = jnp.concatenate([w_hi.astype(F32), w_lo.astype(F32)], axis=0).astype(BF16)
    u = coordinate((WIN - 1) - iota((2 * WIN, 1), 0).astype(F32))
    row_term = u * w0 + shift
    dims = (((1,), (1,)), ((), ()))
    for piece in range(2):
        fixed = []
        for part in range(2):
            e = iota((WIN, 1), 0).astype(F32) + float(part * WIN)
            col_term = coordinate((WIN - 1) - e) * w1
            rows = []
            for i in range(piece * WIN, (piece + 1) * WIN):
                at = (i - part) % (2 * WIN)
                rows.append(jnp.maximum(row_term[at : at + 1, :] + col_term, 0.0))
            h_hi, h_lo = split_two(jnp.concatenate(rows, axis=0))
            both = lax.dot_general(w_both, h_hi, dims, preferred_element_type=F32)
            out = lax.dot_general(w_hi, h_lo, dims, preferred_element_type=F32)
            out = out + both[:heads] + both[heads:]
            value = 16.0 / (1.0 + jnp.exp2(out * -LOG2E)) - CENTRE
            fixed.append(jnp.round(value * FIXED).astype(jnp.int32))
        table_ref[:, piece * 256 : piece * 256 + 256] = (fixed[0] << 16) | (fixed[1] & 0xFFFF)


def expand_head(table_ref, bias_ref, h, mask_add):
    b_row = iota((WIN, 512), 0)
    near = iota((WIN, 512), 1) % WIN <= b_row
    x = jnp.broadcast_to(table_ref[pl.ds(h, 1), :], (WIN, 512))
    r = pltpu.roll(x, 512 - (WIN - 1), 1, stride=1, stride_axis=0)
    strip = jnp.where(near, r, r << 16)
    pair = (strip[:HALF] & -65536) | lax.shift_right_logical(strip[HALF:], 16)
    for a in range(HALF):
        m = 7 - a
        rolled = pair if m == 0 else pltpu.roll(pair, 512 - 16 * m, 1)
        rolled = rolled[:, 0:384]
        first = (rolled >> 16).astype(F32) * (LOG2E / FIXED)
        second = ((rolled << 16) >> 16).astype(F32) * (LOG2E / FIXED)
        if mask_add is not None:
            first = first + mask_add[:HALF]
            second = second + mask_add[HALF:]
        bias_ref[h, a * WIN : a * WIN + HALF, :] = first
        bias_ref[h, a * WIN + HALF : (a + 1) * WIN, :] = second


def bias_expand(table_ref, bias_ref, mask_add):
    @pl.loop(0, HEADS, unroll=8)
    def _(h):
        expand_head(table_ref, bias_ref, h, mask_add)


def project(block, x_rows, w_ref, shift_ref, sharp_ref, q_ref, k_ref, v_ref, beside=None):
    channels = x_rows.shape[1]
    same = (iota((256, 256), 0) // HEAD_DIM == iota((256, 256), 1) // HEAD_DIM).astype(BF16)
    lane_head = iota((1, LANES), 1) // HEAD_DIM
    for piece in range(channels // 256):
        for kind in range(3):
            first = kind * channels + piece * 256
            z = jnp.dot(x_rows, w_ref[:, first : first + 256], preferred_element_type=F32)
            here = slice(piece * 256, piece * 256 + 256)
            if kind == 0:
                z = z + shift_ref[block, 0:1, here]
            if kind == 2:
                z = z + shift_ref[block, 1:2, here]
            else:
                total = jnp.dot((z * z).astype(BF16), same, preferred_element_type=F32)
                z = z * lax.rsqrt(total + EPS_NORM)
            for half in range(2):
                group = piece * 2 + half
                part = z[:, half * LANES : (half + 1) * LANES]
                if kind == 0:
                    scale = jnp.zeros((1, LANES), F32)
                    for j in range(PACK):
                        scale = jnp.where(lane_head == j, sharp_ref[block, group * PACK + j], scale)
                    part = part * (scale * LOG2E)
                target = (q_ref, k_ref, v_ref)[kind]
                target[group] = part.astype(BF16)
            if beside is not None:
                beside(piece * 3 + kind)


def attention(half, q_ref, k_ref, v_ref, bias_ref, ctx_ref):
    lane_head = iota((1, LANES), 1) // HEAD_DIM
    first = half * (TOKENS // 2)
    lanes = slice(128, 384) if half == 0 else slice(0, 256)

    @pl.loop(0, HEADS // PACK, unroll=HEADS // PACK)
    def _(g):
        q = q_ref[g, first : first + TOKENS // 2, :]
        k = k_ref[g]
        v = v_ref[g]
        weights, values = [], []
        for j in range(PACK):
            own = (lane_head == j).astype(BF16)
            scores = lax.dot_general(
                q, k * own, (((1,), (1,)), ((), ())), preferred_element_type=F32
            )
            h = g * PACK + j
            weights.append(jnp.exp2(scores + bias_ref[h, :, lanes]).astype(BF16))
            values.append(jnp.concatenate([v * own, jnp.broadcast_to(own, v.shape)], axis=1))
        both = jnp.dot(
            jnp.concatenate(weights, axis=1),
            jnp.concatenate(values, axis=0),
            preferred_element_type=F32,
        )
        ctx_ref[g, first : first + TOKENS // 2, :] = (both[:, :LANES] / both[:, LANES:]).astype(BF16)


def mix_and_norm(half, block, x_rows, ctx_ref, w_ref, add_ref, gain_ref, shift_ref):
    groups = ctx_ref.shape[0]
    here = slice(half * (TOKENS // 2), (half + 1) * (TOKENS // 2))
    ctx = jnp.concatenate([ctx_ref[g, here, :] for g in range(groups)], axis=1)
    branch = jnp.dot(ctx, w_ref[...], preferred_element_type=F32) + add_ref[block : block + 1, :]
    branch = branch - jnp.mean(branch, axis=-1, keepdims=True)
    spread = jnp.mean(branch * branch, axis=-1, keepdims=True)
    normed = branch * lax.rsqrt(spread + EPS_LAYER)
    x_half = x_rows[here, :].astype(F32)
    return x_half + normed * gain_ref[block : block + 1, :] + shift_ref[block : block + 1, :]


def two_sides(rows):
    grid = rows.reshape(HALF, 2, HALF, rows.shape[1])
    return [jnp.concatenate([grid[r, j] for r in range(HALF)], axis=0) for j in range(2)]


def from_quadrants(parts):
    channels = parts[0].shape[1]
    rows = []
    for i in range(2):
        for r in range(HALF):
            for j in range(2):
                rows.append(parts[2 * i + j][r * HALF : (r + 1) * HALF, :])
    return jnp.concatenate(rows, axis=0)


def body(
    ny,
    nx,
    x_ref,
    w_qkv_hbm,
    qv_shift_ref,
    sharp_ref,
    w_in_ref,
    w_off_ref,
    w_out_ref,
    w_mix_hbm,
    mix_add_ref,
    gain_ref,
    shift_ref,
    out_ref,
    w_qkv_ref,
    w_mix_ref,
    table_ref,
    bias_ref,
    q_ref,
    k_ref,
    v_ref,
    ctx_ref,
    send_ref,
    window_ref,
    back_ref,
    w_sem,
    send_sem,
    recv_sem,
    back_send_sem,
    back_recv_sem,
):
    gy = lax.axis_index("gy")
    gx = lax.axis_index("gx")
    prev_y, next_y = lax.rem(gy + ny - 1, ny), lax.rem(gy + 1, ny)
    prev_x, next_x = lax.rem(gx + nx - 1, nx), lax.rem(gx + 1, nx)
    givers = {1: (gy, prev_x), 2: (prev_y, gx), 3: (prev_y, prev_x)}
    takers = {1: (gy, next_x), 2: (next_y, gx), 3: (next_y, next_x)}

    barrier = pltpu.get_barrier_semaphore()
    for device in list(givers.values()) + list(takers.values()):
        pl.semaphore_signal(barrier, inc=1, device_id=device, device_id_type=MESH)

    loads = []
    for block in range(2):
        loads.append(
            (
                pltpu.make_async_copy(w_qkv_hbm.at[block], w_qkv_ref.at[block], w_sem.at[2 * block]),
                pltpu.make_async_copy(w_mix_hbm.at[block], w_mix_ref.at[block], w_sem.at[2 * block + 1]),
            )
        )
    for pair in loads:
        pair[0].start()
        pair[1].start()

    bias_strips(0, w_in_ref, w_off_ref, w_out_ref, table_ref)

    def some_bias(step):
        for h in range(step * HEADS // 9, (step + 1) * HEADS // 9):
            expand_head(table_ref, bias_ref, h, None)

    loads[0][0].wait()
    x = x_ref[...]
    project(0, x, w_qkv_ref.at[0], qv_shift_ref, sharp_ref, q_ref, k_ref, v_ref, some_bias)
    out_copies = {
        n: pltpu.make_async_remote_copy(
            src_ref=send_ref.at[n - 1],
            dst_ref=window_ref.at[n],
            send_sem=send_sem.at[n - 1],
            recv_sem=recv_sem.at[n - 1],
            device_id=givers[n],
            device_id_type=MESH,
        )
        for n in (1, 2, 3)
    }
    attention(0, q_ref, k_ref, v_ref, bias_ref, ctx_ref)
    loads[0][1].wait()
    mixed = (0, x, ctx_ref, w_mix_ref.at[0], mix_add_ref, gain_ref, shift_ref)
    left, right = two_sides(mix_and_norm(0, *mixed))
    send_ref[2] = left.astype(BF16)
    send_ref[1] = right.astype(BF16)
    pl.semaphore_wait(barrier, 6)
    out_copies[3].start()
    out_copies[2].start()
    attention(1, q_ref, k_ref, v_ref, bias_ref, ctx_ref)
    left, right = two_sides(mix_and_norm(1, *mixed))
    send_ref[0] = left.astype(BF16)
    out_copies[1].start()
    window_ref[0] = right.astype(BF16)

    bias_strips(1, w_in_ref, w_off_ref, w_out_ref, table_ref)
    b_low = iota((WIN, 384), 0) < HALF
    lane = iota((WIN, 384), 1)
    d_low = lane % WIN < HALF
    col_differs = jnp.where(b_low != d_low, 1, 0) * (gx == nx - 1).astype(jnp.int32)
    row_differs = jnp.where((lane < 128) | (lane >= 256), 1, 0) * (gy == ny - 1).astype(jnp.int32)
    mask_add = jnp.where(col_differs + row_differs > 0, -MASK2, 0.0)
    bias_expand(table_ref, bias_ref, mask_add)
    loads[1][0].wait()
    for copy in out_copies.values():
        copy.wait()

    x = from_quadrants([window_ref[n].astype(F32) for n in range(4)]).astype(BF16)
    project(1, x, w_qkv_ref.at[1], qv_shift_ref, sharp_ref, q_ref, k_ref, v_ref)
    back_copies = {
        n: pltpu.make_async_remote_copy(
            src_ref=back_ref.at[n],
            dst_ref=out_ref.at[3 - n],
            send_sem=back_send_sem.at[n],
            recv_sem=back_recv_sem.at[n],
            device_id=takers[n],
            device_id_type=MESH,
        )
        for n in (1, 2, 3)
    }
    attention(1, q_ref, k_ref, v_ref, bias_ref, ctx_ref)
    loads[1][1].wait()
    mixed = (1, x, ctx_ref, w_mix_ref.at[1], mix_add_ref, gain_ref, shift_ref)
    left, right = two_sides(mix_and_norm(1, *mixed))
    back_ref[3] = right.astype(BF16)
    back_copies[3].start()
    back_ref[2] = left.astype(BF16)
    back_copies[2].start()
    attention(0, q_ref, k_ref, v_ref, bias_ref, ctx_ref)
    left, right = two_sides(mix_and_norm(0, *mixed))
    back_ref[1] = right.astype(BF16)
    back_copies[1].start()
    back_ref[0] = left.astype(BF16)
    keep = pltpu.make_async_copy(back_ref.at[0], out_ref.at[3], back_send_sem.at[0])
    keep.start()
    for copy in back_copies.values():
        copy.wait()
    keep.wait()


def on_device(x, w_qkv, qv_shift, sharp, w_in, w_off, w_out, w_mix, mix_add, gain, shift):
    rows, cols, channels = x.shape
    groups = HEADS // PACK
    vmem = pl.BlockSpec(memory_space=pltpu.VMEM)
    smem = pl.BlockSpec(memory_space=pltpu.SMEM)
    hbm = pl.BlockSpec(memory_space=pl.ANY)
    kernel = functools.partial(body, lax.axis_size("gy"), lax.axis_size("gx"))
    out = pl.pallas_call(
        kernel,
        out_shape=jax.ShapeDtypeStruct((4, QUARTER, channels), BF16),
        in_specs=[vmem, hbm, vmem, smem, vmem, vmem, vmem, hbm, vmem, vmem, vmem],
        out_specs=hbm,
        scratch_shapes=[
            pltpu.VMEM(w_qkv.shape, BF16),
            pltpu.VMEM(w_mix.shape, BF16),
            pltpu.VMEM((HEADS, 512), jnp.int32),
            pltpu.VMEM((HEADS, 128, 384), F32),
            pltpu.VMEM((groups, TOKENS, LANES), BF16),
            pltpu.VMEM((groups, TOKENS, LANES), BF16),
            pltpu.VMEM((groups, TOKENS, LANES), BF16),
            pltpu.VMEM((groups, TOKENS, LANES), BF16),
            pltpu.VMEM((3, QUARTER, channels), BF16),
            pltpu.VMEM((4, QUARTER, channels), BF16),
            pltpu.VMEM((4, QUARTER, channels), BF16),
            pltpu.SemaphoreType.DMA((4,)),
            pltpu.SemaphoreType.DMA((3,)),
            pltpu.SemaphoreType.DMA((3,)),
            pltpu.SemaphoreType.DMA((4,)),
            pltpu.SemaphoreType.DMA((4,)),
        ],
        compiler_params=pltpu.CompilerParams(
            collective_id=0, has_side_effects=True, vmem_limit_bytes=56 * 1024 * 1024
        ),
    )(
        x.reshape(rows * cols, channels),
        w_qkv,
        qv_shift,
        sharp,
        w_in,
        w_off,
        jnp.swapaxes(w_out, 1, 2),
        w_mix,
        mix_add,
        gain,
        shift,
    )
    out = out.reshape(2, 2, HALF, HALF, channels).transpose(0, 2, 1, 3, 4)
    return out.reshape(rows, cols, channels)


def solution(mesh):
    in_specs = (P("gy", "gx", None), P(), P(), P(), P(), P(), P(), P(), P(), P(), P())
    return jax.shard_map(
        on_device, mesh=mesh, in_specs=in_specs, out_specs=P("gy", "gx", None), check_vma=False
    )
```

```python
import functools

import jax
import jax.numpy as jnp
from jax import lax
from jax.experimental import pallas as pl
from jax.experimental.pallas import tpu as pltpu
from jax.sharding import PartitionSpec as P

HEADS = 24
WIN = 16
HALF = WIN // 2
TOKENS = WIN * WIN
QUARTER = HALF * HALF
HEAD_DIM = 32
PACK = 4
LANES = PACK * HEAD_DIM
SPAN = 2 * WIN - 1
EPS_NORM = 1e-06
EPS_LAYER = 1e-05
LOG2E = 1.4426950408889634
MASK2 = 100.0 * LOG2E
CENTRE = 8.0
FIXED = 4095.0
MESH = pl.DeviceIdType.MESH
F32 = jnp.float32
BF16 = jnp.bfloat16


def iota(shape, dim):
    return lax.broadcasted_iota(jnp.int32, shape, dim)


def coordinate(offset):
    scaled = offset / (WIN - 1) * 8.0
    magnitude = jnp.log(jnp.abs(scaled) + 1.0) * (LOG2E / 3.0)
    return jnp.where(scaled < 0.0, -magnitude, magnitude)


def split_two(x):
    hi = x.astype(BF16)
    return hi, (x - hi.astype(F32)).astype(BF16)


def bias_strips(block, w_in_ref, w_off_ref, w_out_ref, table_ref):
    w0 = w_in_ref[block, 0:1, :]
    w1 = w_in_ref[block, 1:2, :]
    shift = w_off_ref[block : block + 1, :]
    w_out = w_out_ref[block]
    heads = w_out.shape[0]
    w_hi, w_lo = split_two(w_out)
    w_both = jnp.concatenate([w_hi.astype(F32), w_lo.astype(F32)], axis=0).astype(BF16)
    u = coordinate((WIN - 1) - iota((2 * WIN, 1), 0).astype(F32))
    row_term = u * w0 + shift
    dims = (((1,), (1,)), ((), ()))
    for piece in range(2):
        fixed = []
        for part in range(2):
            e = iota((WIN, 1), 0).astype(F32) + float(part * WIN)
            col_term = coordinate((WIN - 1) - e) * w1
            rows = []
            for i in range(piece * WIN, (piece + 1) * WIN):
                at = (i - part) % (2 * WIN)
                rows.append(jnp.maximum(row_term[at : at + 1, :] + col_term, 0.0))
            h_hi, h_lo = split_two(jnp.concatenate(rows, axis=0))
            both = lax.dot_general(w_both, h_hi, dims, preferred_element_type=F32)
            out = lax.dot_general(w_hi, h_lo, dims, preferred_element_type=F32)
            out = out + both[:heads] + both[heads:]
            value = 16.0 / (1.0 + jnp.exp2(out * -LOG2E)) - CENTRE
            fixed.append(jnp.round(value * FIXED).astype(jnp.int32))
        table_ref[:, piece * 256 : piece * 256 + 256] = (fixed[0] << 16) | (fixed[1] & 0xFFFF)


def expand_head(table_ref, bias_ref, h, mask_add):
    b_row = iota((WIN, 512), 0)
    near = iota((WIN, 512), 1) % WIN <= b_row
    x = jnp.broadcast_to(table_ref[pl.ds(h, 1), :], (WIN, 512))
    r = pltpu.roll(x, 512 - (WIN - 1), 1, stride=1, stride_axis=0)
    strip = jnp.where(near, r, r << 16)
    pair = (strip[:HALF] & -65536) | lax.shift_right_logical(strip[HALF:], 16)
    for a in range(HALF):
        m = 7 - a
        rolled = pair if m == 0 else pltpu.roll(pair, 512 - 16 * m, 1)
        rolled = rolled[:, 0:384]
        first = (rolled >> 16).astype(F32) * (LOG2E / FIXED)
        second = ((rolled << 16) >> 16).astype(F32) * (LOG2E / FIXED)
        if mask_add is not None:
            first = first + mask_add[:HALF]
            second = second + mask_add[HALF:]
        bias_ref[h, a * WIN : a * WIN + HALF, :] = first
        bias_ref[h, a * WIN + HALF : (a + 1) * WIN, :] = second


def bias_expand(table_ref, bias_ref, mask_add):
    @pl.loop(0, HEADS, unroll=8)
    def _(h):
        expand_head(table_ref, bias_ref, h, mask_add)


def project(block, x_rows, w_ref, shift_ref, sharp_ref, q_ref, k_ref, v_ref, beside=None):
    channels = x_rows.shape[1]
    same = (iota((256, 256), 0) // HEAD_DIM == iota((256, 256), 1) // HEAD_DIM).astype(BF16)
    lane_head = iota((1, LANES), 1) // HEAD_DIM
    for piece in range(channels // 256):
        for kind in range(3):
            first = kind * channels + piece * 256
            z = jnp.dot(x_rows, w_ref[:, first : first + 256], preferred_element_type=F32)
            here = slice(piece * 256, piece * 256 + 256)
            if kind == 0:
                z = z + shift_ref[block, 0:1, here]
            if kind == 2:
                z = z + shift_ref[block, 1:2, here]
            else:
                total = jnp.dot((z * z).astype(BF16), same, preferred_element_type=F32)
                z = z * lax.rsqrt(total + EPS_NORM)
            for half in range(2):
                group = piece * 2 + half
                part = z[:, half * LANES : (half + 1) * LANES]
                if kind == 0:
                    scale = jnp.zeros((1, LANES), F32)
                    for j in range(PACK):
                        scale = jnp.where(lane_head == j, sharp_ref[block, group * PACK + j], scale)
                    part = part * (scale * LOG2E)
                target = (q_ref, k_ref, v_ref)[kind]
                target[group] = part.astype(BF16)
            if beside is not None:
                beside(piece * 3 + kind)


def attention(half, q_ref, k_ref, v_ref, bias_ref, ctx_ref):
    lane_head = iota((1, LANES), 1) // HEAD_DIM
    first = half * (TOKENS // 2)
    lanes = slice(128, 384) if half == 0 else slice(0, 256)

    @pl.loop(0, HEADS // PACK, unroll=HEADS // PACK)
    def _(g):
        q = q_ref[g, first : first + TOKENS // 2, :]
        k = k_ref[g]
        v = v_ref[g]
        weights, values = [], []
        for j in range(PACK):
            own = (lane_head == j).astype(BF16)
            scores = lax.dot_general(
                q, k * own, (((1,), (1,)), ((), ())), preferred_element_type=F32
            )
            h = g * PACK + j
            weights.append(jnp.exp2(scores + bias_ref[h, :, lanes]).astype(BF16))
            values.append(jnp.concatenate([v * own, jnp.broadcast_to(own, v.shape)], axis=1))
        both = jnp.dot(
            jnp.concatenate(weights, axis=1),
            jnp.concatenate(values, axis=0),
            preferred_element_type=F32,
        )
        ctx_ref[g, first : first + TOKENS // 2, :] = (both[:, :LANES] / both[:, LANES:]).astype(BF16)


def attention_all(q_ref, k_ref, v_ref, bias_ref, ctx_ref):
    lane_head = iota((1, LANES), 1) // HEAD_DIM

    @pl.loop(0, HEADS // PACK, unroll=HEADS // PACK)
    def _(g):
        q = q_ref[g]
        k = k_ref[g]
        v = v_ref[g]
        weights, values = [], []
        for j in range(PACK):
            own = (lane_head == j).astype(BF16)
            scores = lax.dot_general(
                q, k * own, (((1,), (1,)), ((), ())), preferred_element_type=F32
            )
            h = g * PACK + j
            top = jnp.exp2(scores[:128] + bias_ref[h, :, 128:384]).astype(BF16)
            low = jnp.exp2(scores[128:] + bias_ref[h, :, 0:256]).astype(BF16)
            weights.append(jnp.concatenate([top, low], axis=0))
            values.append(jnp.concatenate([v * own, jnp.broadcast_to(own, v.shape)], axis=1))
        both = jnp.dot(
            jnp.concatenate(weights, axis=1),
            jnp.concatenate(values, axis=0),
            preferred_element_type=F32,
        )
        ctx_ref[g] = (both[:, :LANES] / both[:, LANES:]).astype(BF16)


def mix_and_norm(half, block, x_rows, ctx_ref, w_ref, add_ref, gain_ref, shift_ref):
    groups = ctx_ref.shape[0]
    here = slice(half * (TOKENS // 2), (half + 1) * (TOKENS // 2))
    ctx = jnp.concatenate([ctx_ref[g, here, :] for g in range(groups)], axis=1)
    branch = jnp.dot(ctx, w_ref[...], preferred_element_type=F32) + add_ref[block : block + 1, :]
    branch = branch - jnp.mean(branch, axis=-1, keepdims=True)
    spread = jnp.mean(branch * branch, axis=-1, keepdims=True)
    normed = branch * lax.rsqrt(spread + EPS_LAYER)
    x_half = x_rows[here, :].astype(F32)
    return x_half + normed * gain_ref[block : block + 1, :] + shift_ref[block : block + 1, :]


def two_sides(rows):
    grid = rows.reshape(HALF, 2, HALF, rows.shape[1])
    return [jnp.concatenate([grid[r, j] for r in range(HALF)], axis=0) for j in range(2)]


def from_quadrants(parts):
    channels = parts[0].shape[1]
    rows = []
    for i in range(2):
        for r in range(HALF):
            for j in range(2):
                rows.append(parts[2 * i + j][r * HALF : (r + 1) * HALF, :])
    return jnp.concatenate(rows, axis=0)


def body(
    ny,
    nx,
    x_ref,
    w_qkv_hbm,
    qv_shift_ref,
    sharp_ref,
    w_in_ref,
    w_off_ref,
    w_out_ref,
    w_mix_hbm,
    mix_add_ref,
    gain_ref,
    shift_ref,
    out_ref,
    w_qkv_ref,
    w_mix_ref,
    table_ref,
    bias_ref,
    q_ref,
    k_ref,
    v_ref,
    ctx_ref,
    send_ref,
    window_ref,
    back_ref,
    w_sem,
    send_sem,
    recv_sem,
    back_send_sem,
    back_recv_sem,
):
    gy = lax.axis_index("gy")
    gx = lax.axis_index("gx")
    prev_y, next_y = lax.rem(gy + ny - 1, ny), lax.rem(gy + 1, ny)
    prev_x, next_x = lax.rem(gx + nx - 1, nx), lax.rem(gx + 1, nx)
    givers = {1: (gy, prev_x), 2: (prev_y, gx), 3: (prev_y, prev_x)}
    takers = {1: (gy, next_x), 2: (next_y, gx), 3: (next_y, next_x)}

    barrier = pltpu.get_barrier_semaphore()
    for device in list(givers.values()) + list(takers.values()):
        pl.semaphore_signal(barrier, inc=1, device_id=device, device_id_type=MESH)

    loads = []
    for block in range(2):
        loads.append(
            (
                pltpu.make_async_copy(w_qkv_hbm.at[block], w_qkv_ref.at[block], w_sem.at[2 * block]),
                pltpu.make_async_copy(w_mix_hbm.at[block], w_mix_ref.at[block], w_sem.at[2 * block + 1]),
            )
        )
    loads[0][0].start()

    bias_strips(0, w_in_ref, w_off_ref, w_out_ref, table_ref)

    def some_bias(step):
        for h in range(step * HEADS // 9, (step + 1) * HEADS // 9):
            expand_head(table_ref, bias_ref, h, None)

    loads[0][0].wait()
    loads[0][1].start()
    loads[1][0].start()
    loads[1][1].start()
    x = x_ref[...]
    project(0, x, w_qkv_ref.at[0], qv_shift_ref, sharp_ref, q_ref, k_ref, v_ref, some_bias)
    out_copies = {
        n: pltpu.make_async_remote_copy(
            src_ref=send_ref.at[n - 1],
            dst_ref=window_ref.at[n],
            send_sem=send_sem.at[n - 1],
            recv_sem=recv_sem.at[n - 1],
            device_id=givers[n],
            device_id_type=MESH,
        )
        for n in (1, 2, 3)
    }
    attention_all(q_ref, k_ref, v_ref, bias_ref, ctx_ref)
    loads[0][1].wait()
    mixed = (0, x, ctx_ref, w_mix_ref.at[0], mix_add_ref, gain_ref, shift_ref)
    left, right = two_sides(mix_and_norm(0, *mixed))
    send_ref[2] = left.astype(BF16)
    send_ref[1] = right.astype(BF16)
    pl.semaphore_wait(barrier, 6)
    out_copies[3].start()
    out_copies[2].start()
    left, right = two_sides(mix_and_norm(1, *mixed))
    send_ref[0] = left.astype(BF16)
    out_copies[1].start()
    window_ref[0] = right.astype(BF16)

    bias_strips(1, w_in_ref, w_off_ref, w_out_ref, table_ref)
    b_low = iota((WIN, 384), 0) < HALF
    lane = iota((WIN, 384), 1)
    d_low = lane % WIN < HALF
    col_differs = jnp.where(b_low != d_low, 1, 0) * (gx == nx - 1).astype(jnp.int32)
    row_differs = jnp.where((lane < 128) | (lane >= 256), 1, 0) * (gy == ny - 1).astype(jnp.int32)
    mask_add = jnp.where(col_differs + row_differs > 0, -MASK2, 0.0)
    bias_expand(table_ref, bias_ref, mask_add)
    loads[1][0].wait()
    for copy in out_copies.values():
        copy.wait()

    x = from_quadrants([window_ref[n].astype(F32) for n in range(4)]).astype(BF16)
    project(1, x, w_qkv_ref.at[1], qv_shift_ref, sharp_ref, q_ref, k_ref, v_ref)
    back_copies = {
        n: pltpu.make_async_remote_copy(
            src_ref=back_ref.at[n],
            dst_ref=out_ref.at[3 - n],
            send_sem=back_send_sem.at[n],
            recv_sem=back_recv_sem.at[n],
            device_id=takers[n],
            device_id_type=MESH,
        )
        for n in (1, 2, 3)
    }
    attention(1, q_ref, k_ref, v_ref, bias_ref, ctx_ref)
    loads[1][1].wait()
    mixed = (1, x, ctx_ref, w_mix_ref.at[1], mix_add_ref, gain_ref, shift_ref)
    left, right = two_sides(mix_and_norm(1, *mixed))
    back_ref[3] = right.astype(BF16)
    back_copies[3].start()
    back_ref[2] = left.astype(BF16)
    back_copies[2].start()
    attention(0, q_ref, k_ref, v_ref, bias_ref, ctx_ref)
    left, right = two_sides(mix_and_norm(0, *mixed))
    back_ref[1] = right.astype(BF16)
    back_copies[1].start()
    back_ref[0] = left.astype(BF16)
    keep = pltpu.make_async_copy(back_ref.at[0], out_ref.at[3], back_send_sem.at[0])
    keep.start()
    for copy in back_copies.values():
        copy.wait()
    keep.wait()


def on_device(x, w_qkv, qv_shift, sharp, w_in, w_off, w_out, w_mix, mix_add, gain, shift):
    rows, cols, channels = x.shape
    groups = HEADS // PACK
    vmem = pl.BlockSpec(memory_space=pltpu.VMEM)
    smem = pl.BlockSpec(memory_space=pltpu.SMEM)
    hbm = pl.BlockSpec(memory_space=pl.ANY)
    kernel = functools.partial(body, lax.axis_size("gy"), lax.axis_size("gx"))
    out = pl.pallas_call(
        kernel,
        out_shape=jax.ShapeDtypeStruct((4, QUARTER, channels), BF16),
        in_specs=[vmem, hbm, vmem, smem, vmem, vmem, vmem, hbm, vmem, vmem, vmem],
        out_specs=hbm,
        scratch_shapes=[
            pltpu.VMEM(w_qkv.shape, BF16),
            pltpu.VMEM(w_mix.shape, BF16),
            pltpu.VMEM((HEADS, 512), jnp.int32),
            pltpu.VMEM((HEADS, 128, 384), F32),
            pltpu.VMEM((groups, TOKENS, LANES), BF16),
            pltpu.VMEM((groups, TOKENS, LANES), BF16),
            pltpu.VMEM((groups, TOKENS, LANES), BF16),
            pltpu.VMEM((groups, TOKENS, LANES), BF16),
            pltpu.VMEM((3, QUARTER, channels), BF16),
            pltpu.VMEM((4, QUARTER, channels), BF16),
            pltpu.VMEM((4, QUARTER, channels), BF16),
            pltpu.SemaphoreType.DMA((4,)),
            pltpu.SemaphoreType.DMA((3,)),
            pltpu.SemaphoreType.DMA((3,)),
            pltpu.SemaphoreType.DMA((4,)),
            pltpu.SemaphoreType.DMA((4,)),
        ],
        compiler_params=pltpu.CompilerParams(
            collective_id=0, has_side_effects=True, vmem_limit_bytes=56 * 1024 * 1024
        ),
    )(
        x.reshape(rows * cols, channels),
        w_qkv,
        qv_shift,
        sharp,
        w_in,
        w_off,
        jnp.swapaxes(w_out, 1, 2),
        w_mix,
        mix_add,
        gain,
        shift,
    )
    out = out.reshape(2, 2, HALF, HALF, channels).transpose(0, 2, 1, 3, 4)
    return out.reshape(rows, cols, channels)


def solution(mesh):
    in_specs = (P("gy", "gx", None), P(), P(), P(), P(), P(), P(), P(), P(), P(), P())
    return jax.shard_map(
        on_device, mesh=mesh, in_specs=in_specs, out_specs=P("gy", "gx", None), check_vma=False
    )
```
